32 devices in a mesh: seq: 8 (over y, x, core), head: 4 (over z).
Axes of the slice: x: 2, y: 2, z: 4, core: 2. Of those that a mesh axis runs over, the one named last changes fastest.
Arguments:
- query_rows: bfloat16 [4096, 2048], P('seq', 'head'), may hold values from -18 to 18
- key_rows: bfloat16 [4096, 2048], P('seq', 'head'), may hold values from -18 to 18
- value_rows: bfloat16 [4096, 2048], P('seq', 'head'), may hold values from -6 to 6
- out_grad: bfloat16 [4096, 4096], P('seq', 'head'), may hold values from -6 to 6
- out_weight: bfloat16 [2048, 4096], P('head', 'seq'), may hold values from -0.09375 to 0.09375
Outputs:
- attended: bfloat16 [4096, 2048], P('seq', 'head')
- query_grad: bfloat16 [4096, 2048], P('seq', 'head')
- key_grad: bfloat16 [4096, 2048], P('seq', 'head')
- value_grad: bfloat16 [4096, 2048], P('seq', 'head')
The draws below stay inside these ranges and needn't reach their ends.
All inputs are finite; a program needn't handle non-finite values.
Results may differ from the reference program's by a relative error of at most 0.0067.
Values may be sent and summed in bfloat16 or wider, within the bound.
A program may use at most 64 MiB of HBM per device.

```python
import jax
import jax.numpy as jnp
from jax import lax

D = 4096
HEADS = 16
DH = 128
STRIDE = 512
BLOCK = 128
TOKENS = 4096
N_SEQ = 8


def base_values(key):
    return jnp.clip(jax.random.normal(key, (TOKENS, HEADS * DH), jnp.float32), -6.0, 6.0)


def draw_query_rows(key, part):
    values = base_values(jax.random.fold_in(key, 1))
    return values.astype(jnp.bfloat16)


def draw_key_rows(key, part):
    values = base_values(jax.random.fold_in(key, 2))
    return values.astype(jnp.bfloat16)


def shard_levels(key, extent, cuts, least, largest):
    gain = 1.0
    for axis_at, blocks in cuts:
        heights = jax.random.uniform(jax.random.fold_in(jax.random.fold_in(key, 6), axis_at), (blocks,), jnp.float32, least / len(cuts), largest / len(cuts))
        gain = gain * jnp.repeat(jnp.exp(heights), extent[axis_at] // blocks).reshape((-1,) + (1,) * (len(extent) - 1 - axis_at))
    return gain


def gaussian(key, dims, width, reach, cuts=(), kind=jnp.bfloat16):
    array = jax.random.normal(key, dims, jnp.float32) * width
    if len(cuts) > 0:
        array = shard_levels(key, dims, cuts, -0.22, 0.18) * array
    return jnp.clip(array, min=-reach, max=reach).astype(kind)


def setup_inputs(seed: int = 0) -> dict:
    splits = jax.random.split(jax.random.key(seed), 6)
    query_rows = draw_query_rows(jax.random.fold_in(splits[5], 71), 0)
    key_rows = draw_key_rows(jax.random.fold_in(splits[5], 71), 0)
    value_rows = gaussian(splits[2], (TOKENS, HEADS * DH), 1.0, 6.0, ((0, 8), (1, 4)))
    out_grad = gaussian(splits[3], (TOKENS, D), 1.0, 6.0, ((0, 8), (1, 4)))
    out_weight = gaussian(splits[4], (HEADS * DH, D), D ** -0.5, 0.09375, ((0, 4), (1, 8)))
    return {"query_rows": query_rows, "key_rows": key_rows, "value_rows": value_rows, "out_grad": out_grad, "out_weight": out_weight}


SENTINEL = -1.0e30


def rounded(values):
    return lax.optimization_barrier(values.astype(jnp.bfloat16)).astype(jnp.float32)


def part_forward(queries, keys_part, values_part, visible, layout_forms):
    query_form, key_form, score_form = layout_forms
    scaling = DH ** -0.5
    scores = jnp.einsum(query_form + "," + key_form + "->" + score_form, queries.astype(jnp.float32), keys_part.astype(jnp.float32)) * scaling
    row_max = jnp.max(jnp.where(visible, scores, SENTINEL), axis=-1)
    weights = jnp.where(visible, jnp.exp(scores - row_max[..., None]), 0.0)
    row_sum = jnp.sum(weights, axis=-1)
    partial_out = jnp.einsum(score_form + "," + key_form + "->" + query_form, rounded(weights), values_part.astype(jnp.float32))
    return scores, row_max, row_sum, partial_out


def part_backward(scores, visible, lse_rows, delta_rows, queries, keys_part, values_part, grad_part, layout_forms):
    query_form, key_form, score_form = layout_forms
    scaling = DH ** -0.5
    probs = jnp.where(visible, jnp.exp(scores - lse_rows[..., None]), 0.0)
    value_part_grad = jnp.einsum(score_form + "," + query_form + "->" + key_form, rounded(probs), grad_part.astype(jnp.float32))
    dprob = jnp.einsum(query_form + "," + key_form + "->" + score_form, grad_part.astype(jnp.float32), values_part.astype(jnp.float32))
    dscore = rounded(probs * (dprob - delta_rows[..., None]))
    query_part_grad = jnp.einsum(score_form + "," + key_form + "->" + query_form, dscore, keys_part.astype(jnp.float32)) * scaling
    key_part_grad = jnp.einsum(score_form + "," + query_form + "->" + key_form, dscore, queries.astype(jnp.float32)) * scaling
    return query_part_grad, key_part_grad, value_part_grad


def combine_stats(max_band, sum_band, dot_band, max_strided, sum_strided, dot_strided):
    top = jnp.maximum(max_band, max_strided)
    band_factor = jnp.exp(max_band - top)
    strided_factor = jnp.exp(max_strided - top)
    total = band_factor * sum_band + strided_factor * sum_strided
    delta = (band_factor * dot_band + strided_factor * dot_strided) / total
    return band_factor, strided_factor, total, top + jnp.log(total), delta


def band_view(values):
    return values.reshape(TOKENS // BLOCK, BLOCK, values.shape[-1])


def band_back(values):
    return values.reshape((TOKENS,) + values.shape[2:])


def strided_view(values):
    return jnp.swapaxes(values.reshape((N_SEQ, STRIDE) + values.shape[1:]), 0, 1)


def strided_back(values):
    return jnp.swapaxes(values, 0, 1).reshape((TOKENS,) + values.shape[2:])


def reference(query_rows, key_rows, value_rows, out_grad, out_weight):
    grad_attended = jnp.dot(out_grad, out_weight.T, preferred_element_type=jnp.float32).astype(jnp.bfloat16)
    band_rows = lax.broadcasted_iota(jnp.int32, (BLOCK, BLOCK), 0)
    band_cols = lax.broadcasted_iota(jnp.int32, (BLOCK, BLOCK), 1)
    band_visible = band_cols <= band_rows
    far_rows = lax.broadcasted_iota(jnp.int32, (N_SEQ, N_SEQ), 0)
    far_cols = lax.broadcasted_iota(jnp.int32, (N_SEQ, N_SEQ), 1)
    strided_visible = far_cols < far_rows
    band_forms = ("bid", "bjd", "bij")
    strided_forms = ("sid", "sjd", "sij")

    def one_head(head_index):
        start = (head_index * DH).astype(jnp.int32)
        query_head = lax.dynamic_slice_in_dim(query_rows, start, DH, 1)
        key_head = lax.dynamic_slice_in_dim(key_rows, start, DH, 1)
        value_head = lax.dynamic_slice_in_dim(value_rows, start, DH, 1)
        grad_head = lax.dynamic_slice_in_dim(grad_attended, start, DH, 1)
        band_scores, max_band, sum_band, out_band = part_forward(band_view(query_head), band_view(key_head), band_view(value_head), band_visible, band_forms)
        strided_scores, max_strided, sum_strided, out_strided = part_forward(strided_view(query_head), strided_view(key_head), strided_view(value_head), strided_visible, strided_forms)
        max_band, sum_band, out_band = band_back(max_band), band_back(sum_band), band_back(out_band)
        max_strided, sum_strided, out_strided = strided_back(max_strided), strided_back(sum_strided), strided_back(out_strided)
        grad_float = grad_head.astype(jnp.float32)
        dot_band = jnp.sum(grad_float * out_band, axis=-1)
        dot_strided = jnp.sum(grad_float * out_strided, axis=-1)
        band_factor, strided_factor, total, lse, delta = combine_stats(max_band, sum_band, dot_band, max_strided, sum_strided, dot_strided)
        attended_head = ((band_factor[:, None] * out_band + strided_factor[:, None] * out_strided) / total[:, None]).astype(jnp.bfloat16)
        band_grads = part_backward(band_scores, band_visible, band_view(lse[:, None])[..., 0], band_view(delta[:, None])[..., 0], band_view(query_head), band_view(key_head), band_view(value_head), band_view(grad_head), band_forms)
        strided_grads = part_backward(strided_scores, strided_visible, strided_view(lse), strided_view(delta), strided_view(query_head), strided_view(key_head), strided_view(value_head), strided_view(grad_head), strided_forms)
        results = [attended_head]
        for which in range(3):
            results.append((band_back(band_grads[which]) + rounded(strided_back(strided_grads[which]))).astype(jnp.bfloat16))
        return tuple(results)

    stacked = lax.map(one_head, jnp.arange(HEADS, dtype=jnp.int32))

    def to_rows(values):
        return jnp.swapaxes(values, 0, 1).reshape(TOKENS, HEADS * DH)

    return (to_rows(stacked[0]), to_rows(stacked[1]), to_rows(stacked[2]), to_rows(stacked[3]))
```

```python
import functools

import jax
import jax.experimental.pallas as pl
import jax.experimental.pallas.tpu as pltpu
import jax.numpy as jnp
from jax import lax
from jax.sharding import PartitionSpec as P

DH = 128
BLOCK = 128


SENTINEL = -1e30


def part_forward(queries, keys_part, values_part, visible, scaling, layout_forms):
    query_form, key_form, score_form, row_order, score_order = layout_forms
    scores = (
        jnp.einsum(
            query_form + "," + key_form + "->" + score_form,
            queries,
            keys_part,
            preferred_element_type=jnp.float32,
        )
        * scaling
    )
    row_max = jnp.max(jnp.where(visible, scores, SENTINEL), axis=-1)
    weights = jnp.where(visible, jnp.exp(scores - row_max[..., None]), 0.0)
    row_sum = jnp.sum(weights, axis=-1)
    partial_out = jnp.einsum(
        score_form + "," + key_form + "->" + query_form,
        weights.astype(jnp.bfloat16),
        values_part,
        preferred_element_type=jnp.float32,
    )
    return (
        scores,
        jnp.transpose(row_max, row_order),
        jnp.transpose(row_sum, row_order),
        partial_out,
    )


def part_backward(
    scores,
    visible,
    lse_rows,
    delta_rows,
    queries,
    keys_part,
    values_part,
    grad_part,
    scaling,
    layout_forms,
):
    query_form, key_form, score_form, row_order, score_order = layout_forms
    probs = jnp.where(
        visible, jnp.exp(scores - jnp.transpose(lse_rows, score_order)[..., None]), 0.0
    )
    value_part_grad = jnp.einsum(
        score_form + "," + query_form + "->" + key_form,
        probs.astype(jnp.bfloat16),
        grad_part,
        preferred_element_type=jnp.float32,
    )
    dprob = jnp.einsum(
        query_form + "," + key_form + "->" + score_form,
        grad_part,
        values_part,
        preferred_element_type=jnp.float32,
    )
    dscore = (probs * (dprob - jnp.transpose(delta_rows, score_order)[..., None])).astype(
        jnp.bfloat16
    )
    query_part_grad = (
        jnp.einsum(
            score_form + "," + key_form + "->" + query_form,
            dscore,
            keys_part,
            preferred_element_type=jnp.float32,
        )
        * scaling
    )
    key_part_grad = (
        jnp.einsum(
            score_form + "," + query_form + "->" + key_form,
            dscore,
            queries,
            preferred_element_type=jnp.float32,
        )
        * scaling
    )
    return (query_part_grad, key_part_grad, value_part_grad)


def combine_stats(max_band, sum_band, dot_band, max_strided, sum_strided, dot_strided):
    top = jnp.maximum(max_band, max_strided)
    band_factor = jnp.exp(max_band - top)
    strided_factor = jnp.exp(max_strided - top)
    total = band_factor * sum_band + strided_factor * sum_strided
    delta = (band_factor * dot_band + strided_factor * dot_strided) / total
    return (band_factor, strided_factor, total, top + jnp.log(total), delta)


def local(query_rows, key_rows, value_rows, out_grad, out_weight):
    tokens_here, width_here = query_rows.shape
    heads_here = width_here // DH
    groups = lax.axis_size("seq")
    residues = tokens_here // groups
    blocks_here = tokens_here // BLOCK
    scaling = DH ** (-0.5)
    band_forms = ("bihd", "bjhd", "bhij", (0, 2, 1), (0, 2, 1))
    strided_forms = ("ishd", "jshd", "shij", (2, 0, 1), (1, 2, 0))
    band_rows = lax.broadcasted_iota(jnp.int32, (BLOCK, BLOCK), 0)
    band_cols = lax.broadcasted_iota(jnp.int32, (BLOCK, BLOCK), 1)
    band_visible = band_cols <= band_rows
    far_rows = lax.broadcasted_iota(jnp.int32, (groups, groups), 0)
    far_cols = lax.broadcasted_iota(jnp.int32, (groups, groups), 1)
    strided_visible = far_cols < far_rows

    def band_view(values):
        return values.reshape(blocks_here, BLOCK, heads_here, DH)

    def group_view(values):
        return values.reshape(groups, residues, width_here)

    def strided_view(values):
        return values.reshape(groups, residues, heads_here, DH)

    full_grad = lax.all_gather(out_grad, "head", axis=1, tiled=True)
    grad_rows = lax.dot_general(
        full_grad,
        lax.all_gather(out_weight, "seq", axis=1, tiled=True),
        (((1,), (1,)), ((), ())),
        preferred_element_type=jnp.float32,
    ).astype(jnp.bfloat16)
    strided_query, strided_key, strided_value, strided_grad = (
        lax.all_to_all(group_view(query_rows), "seq", split_axis=0, concat_axis=0, tiled=True),
        lax.all_to_all(group_view(key_rows), "seq", split_axis=0, concat_axis=0, tiled=True),
        lax.all_to_all(group_view(value_rows), "seq", split_axis=0, concat_axis=0, tiled=True),
        lax.all_to_all(group_view(grad_rows), "seq", split_axis=0, concat_axis=0, tiled=True),
    )
    query_band = band_view(query_rows)
    key_band = band_view(key_rows)
    value_band = band_view(value_rows)
    band_scores, max_band, sum_band, out_band = part_forward(
        query_band, key_band, value_band, band_visible, scaling, band_forms
    )
    max_band = max_band.reshape(tokens_here, heads_here)
    sum_band = sum_band.reshape(tokens_here, heads_here)
    out_band = out_band.reshape(tokens_here, heads_here, DH)
    grad_heads = grad_rows.reshape(tokens_here, heads_here, DH)
    dot_band = jnp.sum(grad_heads.astype(jnp.float32) * out_band, axis=-1)
    far_query = strided_view(strided_query)
    far_key = strided_view(strided_key)
    far_value = strided_view(strided_value)
    far_scores, max_far, sum_far, out_far = part_forward(
        far_query, far_key, far_value, strided_visible, scaling, strided_forms
    )
    max_band_split = max_band.reshape(groups, residues, heads_here)
    sum_band_split = sum_band.reshape(groups, residues, heads_here)
    dot_band_split = dot_band.reshape(groups, residues, heads_here)
    home_out, home_max, home_sum, band_max_far, band_sum_far, band_dot_far = (
        lax.all_to_all(out_far, "seq", split_axis=0, concat_axis=0, tiled=True),
        lax.all_to_all(max_far, "seq", split_axis=0, concat_axis=0, tiled=True),
        lax.all_to_all(sum_far, "seq", split_axis=0, concat_axis=0, tiled=True),
        lax.all_to_all(max_band_split, "seq", split_axis=0, concat_axis=0, tiled=True),
        lax.all_to_all(sum_band_split, "seq", split_axis=0, concat_axis=0, tiled=True),
        lax.all_to_all(dot_band_split, "seq", split_axis=0, concat_axis=0, tiled=True),
    )
    home_out = home_out.reshape(tokens_here, heads_here, DH)
    home_max = home_max.reshape(tokens_here, heads_here)
    home_sum = home_sum.reshape(tokens_here, heads_here)
    home_dot = jnp.sum(grad_heads.astype(jnp.float32) * home_out, axis=-1)
    band_factor, far_factor, total, lse_home, delta_home = combine_stats(
        max_band, sum_band, dot_band, home_max, home_sum, home_dot
    )
    attended = (
        ((band_factor[..., None] * out_band + far_factor[..., None] * home_out) / total[..., None])
        .astype(jnp.bfloat16)
        .reshape(tokens_here, width_here)
    )
    far_grad = strided_view(strided_grad)
    far_dot = jnp.sum(far_grad.astype(jnp.float32) * out_far, axis=-1)
    far_stats = combine_stats(band_max_far, band_sum_far, band_dot_far, max_far, sum_far, far_dot)
    band_grads = part_backward(
        band_scores,
        band_visible,
        lse_home.reshape(blocks_here, BLOCK, heads_here),
        delta_home.reshape(blocks_here, BLOCK, heads_here),
        query_band,
        key_band,
        value_band,
        band_view(grad_rows),
        scaling,
        band_forms,
    )
    far_grads = part_backward(
        far_scores,
        strided_visible,
        far_stats[3],
        far_stats[4],
        far_query,
        far_key,
        far_value,
        far_grad,
        scaling,
        strided_forms,
    )
    home_query, home_key, home_value = (
        lax.all_to_all(
            far_grads[0].astype(jnp.bfloat16).reshape(groups, residues, width_here),
            "seq",
            split_axis=0,
            concat_axis=0,
            tiled=True,
        ),
        lax.all_to_all(
            far_grads[1].astype(jnp.bfloat16).reshape(groups, residues, width_here),
            "seq",
            split_axis=0,
            concat_axis=0,
            tiled=True,
        ),
        lax.all_to_all(
            far_grads[2].astype(jnp.bfloat16).reshape(groups, residues, width_here),
            "seq",
            split_axis=0,
            concat_axis=0,
            tiled=True,
        ),
    )
    query_grad = (
        band_grads[0].reshape(tokens_here, width_here)
        + home_query.reshape(tokens_here, width_here).astype(jnp.float32)
    ).astype(jnp.bfloat16)
    key_grad = (
        band_grads[1].reshape(tokens_here, width_here)
        + home_key.reshape(tokens_here, width_here).astype(jnp.float32)
    ).astype(jnp.bfloat16)
    value_grad = (
        band_grads[2].reshape(tokens_here, width_here)
        + home_value.reshape(tokens_here, width_here).astype(jnp.float32)
    ).astype(jnp.bfloat16)
    return (attended, query_grad, key_grad, value_grad)


MESH = pl.DeviceIdType.MESH
STAT = 128
ROWS = 16


def dot_nt(a, b):
    return lax.dot_general(a, b, (((1,), (1,)), ((), ())), preferred_element_type=jnp.float32)


def dot_nn(a, b):
    return lax.dot_general(a, b, (((1,), (0,)), ((), ())), preferred_element_type=jnp.float32)


def dot_tn(a, b):
    return lax.dot_general(a, b, (((0,), (0,)), ((), ())), preferred_element_type=jnp.float32)


def pack_stats(columns):
    rows = columns[0].shape[0]
    lane = lax.broadcasted_iota(jnp.int32, (rows, STAT), 1)
    which = lane % 8
    spread = jnp.zeros((rows, STAT), jnp.float32)
    for index, column in enumerate(columns):
        spread = jnp.where(which == index, column, spread)
    first = spread.astype(jnp.bfloat16).astype(jnp.float32)
    rest = spread - first
    second = rest.astype(jnp.bfloat16).astype(jnp.float32)
    third = rest - second
    packed = jnp.where(lane < 8, first, jnp.where(lane < 16, second, jnp.where(lane < 24, third, 0.0)))
    return packed.astype(jnp.bfloat16)


def unpack_stat(packed, index):
    lane = lax.broadcasted_iota(jnp.int32, packed.shape, 1)
    return jnp.sum(jnp.where(lane % 8 == index, packed, 0.0), axis=1, keepdims=True)


def fused_kernel(
    groups, heads, chunks, planes,
    q, k, v, og, w,
    att_out, dq_out, dk_out, dv_out,
    og_all, w_all, qf, kf, vf, g_home, gf, far_out, home_out, gr_send, gr_home,
    out_band, att_full, lse_keep, s_band, s_far, band_grads,
    z_send, z_recv, w_send, w_recv, qkv_send, qkv_recv, out_send, out_recv,
    g_send, g_recv, gr_ssem, gr_rsem,
):
    s = lax.axis_index("seq")
    h = lax.axis_index("head")
    width = heads * DH
    scaling = DH ** (-0.5)
    blocks = groups // 2
    block_rows = groups * ROWS
    row = lax.broadcasted_iota(jnp.int32, (block_rows, block_rows), 0)
    col = lax.broadcasted_iota(jnp.int32, (block_rows, block_rows), 1)
    band_mask = col <= row
    far_mask = (row % ROWS == col % ROWS) & (col // ROWS < row // ROWS)

    def remote(src, dst, ssem, rsem, to):
        return pltpu.make_async_remote_copy(
            src_ref=src, dst_ref=dst, send_sem=ssem, recv_sem=rsem, device_id=to, device_id_type=MESH
        )

    core, x, y = s % 2, s // 2 % 2, s // 4

    def other(o):
        return (
            (1 - y if o & 4 else y) * 4 + (1 - x if o & 2 else x) * 2 + (1 - core if o & 1 else core)
        )

    def peer(o):
        return (other(o), h)

    barrier = pltpu.get_barrier_semaphore()
    for o in range(1, groups):
        pl.semaphore_signal(barrier, inc=1, device_id=peer(o), device_id_type=MESH)
    for z in range(planes):
        @pl.when((h == z + 1) | (h == z - 1))
        def _():
            pl.semaphore_signal(barrier, inc=1, device_id=(s, z), device_id_type=MESH)
    inner = (h > 0) & (h < planes - 1)

    @pl.when(inner)
    def _():
        pl.semaphore_wait(barrier, groups + 1)

    @pl.when(jnp.logical_not(inner))
    def _():
        pl.semaphore_wait(barrier, groups)

    def z_copy(slot, c, direction):
        mine = og_all.at[slot, c]
        return remote(mine, mine, z_send.at[direction, slot, c], z_recv.at[slot, c],
                      (s, h + (1 if direction == 0 else -1)))

    def z_own(c, direction):
        return remote(og.at[:, c], og_all.at[h, c], z_send.at[direction, h, c], z_recv.at[h, c],
                      (s, h + (1 if direction == 0 else -1)))

    def z_pass(slot, c):
        @pl.when(h != slot)
        def _():
            z_copy(slot, c, 0).wait_recv()

        @pl.when((h > slot) & (h < planes - 1))
        def _():
            z_copy(slot, c, 0).start()

        @pl.when((h < slot) & (h > 0))
        def _():
            z_copy(slot, c, 1).start()

    @pl.loop(0, chunks)
    def _(c):
        @pl.when(h < planes - 1)
        def _():
            z_own(c, 0).start()

        @pl.when(h > 0)
        def _():
            z_own(c, 1).start()

    half = w.shape[0] // 2
    low, high = pl.ds(0, half), pl.ds(half, half)

    def w_own(index, o):
        return remote(w, w_all.at[s], w_send.at[index], w_recv.at[index], peer(o))

    def w_part(index, source, rows, o):
        ref = w_all.at[source, rows]
        return remote(ref, ref, w_send.at[index], w_recv.at[index], peer(o))

    w_first = [w_own(0, 2), w_own(1, 4), w_own(2, 1)]
    for copy in w_first:
        copy.start()

    def qkv_copy(t, src, dst, o):
        return remote(src.at[other(o)], dst.at[:, s], qkv_send.at[t, o], qkv_recv.at[t, o], peer(o))

    triples = ((q, qf), (k, kf), (v, vf))
    for o in (6, 2, 4, 7, 3, 5, 1):
        for t, (src, dst) in enumerate(triples):
            qkv_copy(t, src, dst, o).start()
    for src, dst in triples:
        dst[:, s] = src[s]
    w_all[s] = w[...]

    def forward_block(queries, keys_part, values_part, mask):
        scores = dot_nt(queries, keys_part) * scaling
        row_max = jnp.max(jnp.where(mask, scores, SENTINEL), axis=1, keepdims=True)
        weights = jnp.where(mask, jnp.exp(scores - row_max), 0.0)
        row_sum = jnp.maximum(jnp.sum(weights, axis=1, keepdims=True), 1.0)
        partial = dot_nn(weights.astype(jnp.bfloat16), values_part) / row_sum
        return scores, row_max + jnp.log(row_sum), partial

    def columns(head):
        return slice(head * DH, (head + 1) * DH)

    def natural(ref, b):
        return ref[pl.ds(2 * b, 2)].reshape(block_rows, ref.shape[-1])

    def place(column, head, rows):
        lane = lax.broadcasted_iota(jnp.int32, (rows, STAT), 1)
        return jnp.where(lane == head, column, 0.0)

    @pl.loop(0, blocks)
    def _(b):
        qb, kb, vb = natural(q, b), natural(k, b), natural(v, b)
        kept = jnp.zeros((block_rows, STAT), jnp.float32)
        for head in range(heads):
            at = columns(head)
            scores, lse, partial = forward_block(qb[:, at], kb[:, at], vb[:, at], band_mask)
            s_band[b * heads + head] = scores
            out_band[b, :, at] = partial
            kept = kept + place(lse, head, block_rows)
        lse_keep[pl.ds(2 * b, 2)] = kept.reshape(2, chunks, ROWS, STAT)

    w_own(0, 2).wait_recv()
    w_second = [w_part(3, other(2), low, 4), w_part(4, other(2), slice(None), 1)]
    for copy in w_second:
        copy.start()
    w_own(1, 4).wait_recv()
    w_third = [w_part(5, other(4), high, 2), w_part(6, other(4), slice(None), 1)]
    for copy in w_third:
        copy.start()

    def z_near(c):
        for slot in range(planes):
            @pl.when((h == slot + 1) | (h == slot - 1))
            def _():
                z_pass(slot, c)

    def z_far(c):
        for distance in range(2, planes):
            for slot in range(planes):
                @pl.when((h == slot + distance) | (h == slot - distance))
                def _():
                    z_pass(slot, c)

    @pl.loop(0, chunks)
    def _(c):
        z_near(c)

    w_part(3, other(6), low, 4).wait_recv()
    w_fourth = [w_part(7, other(6), low, 1)]
    w_fourth[0].start()
    w_part(5, other(6), high, 2).wait_recv()
    w_fourth.append(w_part(8, other(6), high, 1))
    w_fourth[1].start()

    for o in range(1, groups):
        for t, (src, dst) in enumerate(triples):
            qkv_copy(t, src, dst, o).wait_recv()

    def out_copy(c, o):
        return remote(far_out.at[c, other(o)], home_out.at[s, c], out_send.at[c, o], out_recv.at[c, o], peer(o))

    def out_arrived(c, o):
        return remote(far_out.at[c, other(o)], home_out.at[other(o), c], out_send.at[c, o], out_recv.at[c, o], peer(o))

    def chunk_of(ref, c):
        return ref[c].reshape(block_rows, ref.shape[-1])

    @pl.loop(0, chunks)
    def _(c):
        qb, kb, vb = chunk_of(qf, c), chunk_of(kf, c), chunk_of(vf, c)
        stats = []
        for head in range(heads):
            at = columns(head)
            scores, lse, partial = forward_block(qb[:, at], kb[:, at], vb[:, at], far_mask)
            s_far[c * heads + head] = scores
            far_out[c, :, :, at] = partial.astype(jnp.bfloat16).reshape(groups, ROWS, DH)
            stats.append(lse)
        far_out[c, :, :, width:] = pack_stats(stats).reshape(groups, ROWS, STAT)
        for o in range(1, groups):
            out_copy(c, o).start()
        home_out[s, c] = far_out[c, s]

    @pl.loop(0, chunks)
    def _(c):
        @pl.when(inner)
        def _():
            z_far(c)

    w_own(2, 1).wait_recv()
    w_part(4, other(3), slice(None), 1).wait_recv()
    w_part(6, other(5), slice(None), 1).wait_recv()
    w_part(7, other(7), low, 1).wait_recv()
    w_part(8, other(7), high, 1).wait_recv()

    @pl.loop(0, chunks)
    def _(c):
        for o in range(1, groups):
            out_arrived(c, o).wait_recv()

    @pl.loop(0, blocks)
    def _(b):
        message = natural(home_out, b)
        packed = message[:, width:].astype(jnp.float32)
        band = natural(lse_keep, b)
        kept = jnp.zeros((block_rows, STAT), jnp.float32)
        for head in range(heads):
            at = columns(head)
            lse_far = unpack_stat(packed, head)
            lse_near = band[:, head:head + 1]
            top = jnp.maximum(lse_far, lse_near)
            near_factor = jnp.exp(lse_near - top)
            far_factor = jnp.exp(lse_far - top)
            total = near_factor + far_factor
            combined = (near_factor * out_band[b, :, at] + far_factor * message[:, at].astype(jnp.float32)) / total
            att_full[pl.ds(2 * b, 2), :, :, at] = combined.reshape(2, chunks, ROWS, DH)
            att_out[pl.ds(2 * b, 2), :, :, at] = combined.astype(jnp.bfloat16).reshape(2, chunks, ROWS, DH)
            kept = kept + place(top + jnp.log(total), head, block_rows)
        lse_keep[pl.ds(2 * b, 2)] = kept.reshape(2, chunks, ROWS, STAT)

    def g_copy(c, o):
        return remote(g_home.at[other(o), c], gf.at[c, s], g_send.at[c, o], g_recv.at[c, o], peer(o))

    def g_arrived(c, o):
        return remote(g_home.at[other(o), c], gf.at[c, other(o)], g_send.at[c, o], g_recv.at[c, o], peer(o))

    def gr_copy(c, o):
        return remote(gr_send.at[c, other(o)], gr_home.at[s, c], gr_ssem.at[c, o], gr_rsem.at[c, o], peer(o))

    def gr_arrived(c, o):
        return remote(gr_send.at[c, other(o)], gr_home.at[other(o), c], gr_ssem.at[c, o], gr_rsem.at[c, o], peer(o))

    @pl.loop(0, chunks)
    def _(c):
        og_all[h, c] = og[:, c]

    def grad_chunk(c):
        @pl.when(jnp.logical_not(inner))
        def _():
            z_far(c)
        total = jnp.zeros((block_rows, width), jnp.float32)
        depth = w.shape[1]
        for source in range(groups):
            per = og.shape[-1] // depth
            left = og_all[source // per, c, :, :, (source % per) * depth:(source % per + 1) * depth]
            total = total + dot_nt(left.reshape(block_rows, depth), w_all[source])
        grad = total.astype(jnp.bfloat16)
        g_home[:, c, :, :width] = grad.reshape(groups, ROWS, width)
        grad = grad.astype(jnp.float32)
        attended = att_full[:, c].reshape(block_rows, width)
        kept = lse_keep[:, c].reshape(block_rows, STAT)
        stats = [kept[:, head:head + 1] for head in range(heads)]
        stats += [jnp.sum(grad[:, columns(head)] * attended[:, columns(head)], axis=1, keepdims=True) for head in range(heads)]
        g_home[:, c, :, width:] = pack_stats(stats).reshape(groups, ROWS, STAT)
        for o in range(1, groups):
            g_copy(c, o).start()
        gf[c, s] = g_home[s, c]

    def backward_block(scores, mask, lse, delta, queries, keys_part, values_part, grad_part):
        probs = jnp.where(mask, jnp.exp(scores - lse), 0.0)
        value_part = dot_tn(probs.astype(jnp.bfloat16), grad_part)
        dprob = dot_nt(grad_part, values_part)
        dscore = (probs * (dprob - delta)).astype(jnp.bfloat16)
        return dot_nn(dscore, keys_part) * scaling, dot_tn(dscore, queries) * scaling, value_part

    def far_backward(c):
        for o in range(1, groups):
            g_arrived(c, o).wait_recv()
        qb, kb, vb, message = chunk_of(qf, c), chunk_of(kf, c), chunk_of(vf, c), chunk_of(gf, c)
        packed = message[:, width:].astype(jnp.float32)
        for head in range(heads):
            at = columns(head)
            parts = backward_block(
                s_far[c * heads + head], far_mask, unpack_stat(packed, head), unpack_stat(packed, heads + head),
                qb[:, at], kb[:, at], vb[:, at], message[:, at],
            )
            for t, part in enumerate(parts):
                gr_send[c, :, t, :, at] = part.astype(jnp.bfloat16).reshape(groups, ROWS, DH)
        for o in range(1, groups):
            gr_copy(c, o).start()
        gr_home[s, c] = gr_send[c, s]

    @pl.loop(0, chunks + 1)
    def _(c):
        @pl.when(c < chunks)
        def _():
            grad_chunk(c)

        @pl.when(c > 0)
        def _():
            far_backward(c - 1)

    @pl.loop(0, blocks)
    def _(b):
        qb, kb, vb, message = natural(q, b), natural(k, b), natural(v, b), natural(g_home, b)
        packed = message[:, width:].astype(jnp.float32)
        for head in range(heads):
            at = columns(head)
            parts = backward_block(
                s_band[b * heads + head], band_mask, unpack_stat(packed, head), unpack_stat(packed, heads + head),
                qb[:, at], kb[:, at], vb[:, at], message[:, at],
            )
            for t, part in enumerate(parts):
                band_grads[t, b, :, at] = part

    @pl.loop(0, chunks)
    def _(c):
        for o in range(1, groups):
            gr_arrived(c, o).wait_recv()

    @pl.loop(0, blocks)
    def _(b):
        for t, result in enumerate((dq_out, dk_out, dv_out)):
            arrived = gr_home[pl.ds(2 * b, 2), :, t].reshape(block_rows, width).astype(jnp.float32)
            result[pl.ds(2 * b, 2)] = (
                (band_grads[t, b] + arrived).astype(jnp.bfloat16).reshape(2, chunks, ROWS, width)
            )

    for copy in w_first + w_second + w_third + w_fourth:
        copy.wait_send()
    for o in range(1, groups):
        for t, (src, dst) in enumerate(triples):
            qkv_copy(t, src, dst, o).wait_send()

    @pl.loop(0, chunks)
    def _(c):
        for o in range(1, groups):
            out_copy(c, o).wait_send()
            g_copy(c, o).wait_send()
            gr_copy(c, o).wait_send()

        @pl.when(h < planes - 1)
        def _():
            z_own(c, 0).wait_send()

        @pl.when(h > 0)
        def _():
            z_own(c, 1).wait_send()

        for slot in range(planes):
            @pl.when((h > slot) & (h < planes - 1))
            def _():
                z_copy(slot, c, 0).wait_send()

            @pl.when((h < slot) & (h > 0))
            def _():
                z_copy(slot, c, 1).wait_send()


def fused_local(query_rows, key_rows, value_rows, out_grad, out_weight):
    tokens_here, width = query_rows.shape
    heads = width // DH
    groups = lax.axis_size("seq")
    planes = lax.axis_size("head")
    chunks = tokens_here // groups // ROWS
    depth = out_grad.shape[1]
    block_rows = groups * ROWS
    blocks = tokens_here // block_rows

    def split(values):
        return values.reshape(groups, chunks, ROWS, values.shape[1])

    half, full = jnp.bfloat16, jnp.float32
    dma = pltpu.SemaphoreType.DMA
    in_vmem = pl.BlockSpec(memory_space=pltpu.VMEM)
    results = pl.pallas_call(
        functools.partial(fused_kernel, groups, heads, chunks, planes),
        out_shape=[jax.ShapeDtypeStruct((groups, chunks, ROWS, width), half)] * 4,
        in_specs=[in_vmem] * 5,
        out_specs=[in_vmem] * 4,
        scratch_shapes=[
            pltpu.VMEM((planes, chunks, groups, ROWS, depth), half),
            pltpu.VMEM((groups,) + out_weight.shape, half),
            pltpu.VMEM((chunks, groups, ROWS, width), half),
            pltpu.VMEM((chunks, groups, ROWS, width), half),
            pltpu.VMEM((chunks, groups, ROWS, width), half),
            pltpu.VMEM((groups, chunks, ROWS, width + STAT), half),
            pltpu.VMEM((chunks, groups, ROWS, width + STAT), half),
            pltpu.VMEM((chunks, groups, ROWS, width + STAT), half),
            pltpu.VMEM((groups, chunks, ROWS, width + STAT), half),
            pltpu.VMEM((chunks, groups, 3, ROWS, width), half),
            pltpu.VMEM((groups, chunks, 3, ROWS, width), half),
            pltpu.VMEM((blocks, block_rows, width), full),
            pltpu.VMEM((groups, chunks, ROWS, width), full),
            pltpu.VMEM((groups, chunks, ROWS, STAT), full),
            pltpu.VMEM((blocks * heads, block_rows, block_rows), full),
            pltpu.VMEM((chunks * heads, block_rows, block_rows), full),
            pltpu.VMEM((3, blocks, block_rows, width), full),
            dma((2, planes, chunks)),
            dma((planes, chunks)),
            dma((9,)),
            dma((9,)),
            dma((3, groups)),
            dma((3, groups)),
            dma((chunks, groups)),
            dma((chunks, groups)),
            dma((chunks, groups)),
            dma((chunks, groups)),
            dma((chunks, groups)),
            dma((chunks, groups)),
        ],
        compiler_params=pltpu.CompilerParams(
            collective_id=0, has_side_effects=True, vmem_limit_bytes=56 << 20
        ),
    )(split(query_rows), split(key_rows), split(value_rows), split(out_grad), out_weight)
    return tuple(result.reshape(tokens_here, width) for result in results)


def fits(mesh):
    return mesh.shape["seq"] == 8 and mesh.shape["head"] == 4


def solution(mesh):
    placed = (
        P("seq", "head"),
        P("seq", "head"),
        P("seq", "head"),
        P("seq", "head"),
        P("head", "seq"),
    )
    return jax.shard_map(
        fused_local if fits(mesh) else local,
        mesh=mesh,
        in_specs=placed,
        out_specs=(P("seq", "head"), P("seq", "head"), P("seq", "head"), P("seq", "head")),
        check_vma=False,
    )
```

```python
import functools

import jax
import jax.experimental.pallas as pl
import jax.experimental.pallas.tpu as pltpu
import jax.numpy as jnp
from jax import lax
from jax.sharding import PartitionSpec as P

DH = 128
BLOCK = 128


SENTINEL = -1e30


def part_forward(queries, keys_part, values_part, visible, scaling, layout_forms):
    query_form, key_form, score_form, row_order, score_order = layout_forms
    scores = (
        jnp.einsum(
            query_form + "," + key_form + "->" + score_form,
            queries,
            keys_part,
            preferred_element_type=jnp.float32,
        )
        * scaling
    )
    row_max = jnp.max(jnp.where(visible, scores, SENTINEL), axis=-1)
    weights = jnp.where(visible, jnp.exp(scores - row_max[..., None]), 0.0)
    row_sum = jnp.sum(weights, axis=-1)
    partial_out = jnp.einsum(
        score_form + "," + key_form + "->" + query_form,
        weights.astype(jnp.bfloat16),
        values_part,
        preferred_element_type=jnp.float32,
    )
    return (
        scores,
        jnp.transpose(row_max, row_order),
        jnp.transpose(row_sum, row_order),
        partial_out,
    )


def part_backward(
    scores,
    visible,
    lse_rows,
    delta_rows,
    queries,
    keys_part,
    values_part,
    grad_part,
    scaling,
    layout_forms,
):
    query_form, key_form, score_form, row_order, score_order = layout_forms
    probs = jnp.where(
        visible, jnp.exp(scores - jnp.transpose(lse_rows, score_order)[..., None]), 0.0
    )
    value_part_grad = jnp.einsum(
        score_form + "," + query_form + "->" + key_form,
        probs.astype(jnp.bfloat16),
        grad_part,
        preferred_element_type=jnp.float32,
    )
    dprob = jnp.einsum(
        query_form + "," + key_form + "->" + score_form,
        grad_part,
        values_part,
        preferred_element_type=jnp.float32,
    )
    dscore = (probs * (dprob - jnp.transpose(delta_rows, score_order)[..., None])).astype(
        jnp.bfloat16
    )
    query_part_grad = (
        jnp.einsum(
            score_form + "," + key_form + "->" + query_form,
            dscore,
            keys_part,
            preferred_element_type=jnp.float32,
        )
        * scaling
    )
    key_part_grad = (
        jnp.einsum(
            score_form + "," + query_form + "->" + key_form,
            dscore,
            queries,
            preferred_element_type=jnp.float32,
        )
        * scaling
    )
    return (query_part_grad, key_part_grad, value_part_grad)


def combine_stats(max_band, sum_band, dot_band, max_strided, sum_strided, dot_strided):
    top = jnp.maximum(max_band, max_strided)
    band_factor = jnp.exp(max_band - top)
    strided_factor = jnp.exp(max_strided - top)
    total = band_factor * sum_band + strided_factor * sum_strided
    delta = (band_factor * dot_band + strided_factor * dot_strided) / total
    return (band_factor, strided_factor, total, top + jnp.log(total), delta)


def local(query_rows, key_rows, value_rows, out_grad, out_weight):
    tokens_here, width_here = query_rows.shape
    heads_here = width_here // DH
    groups = lax.axis_size("seq")
    residues = tokens_here // groups
    blocks_here = tokens_here // BLOCK
    scaling = DH ** (-0.5)
    band_forms = ("bihd", "bjhd", "bhij", (0, 2, 1), (0, 2, 1))
    strided_forms = ("ishd", "jshd", "shij", (2, 0, 1), (1, 2, 0))
    band_rows = lax.broadcasted_iota(jnp.int32, (BLOCK, BLOCK), 0)
    band_cols = lax.broadcasted_iota(jnp.int32, (BLOCK, BLOCK), 1)
    band_visible = band_cols <= band_rows
    far_rows = lax.broadcasted_iota(jnp.int32, (groups, groups), 0)
    far_cols = lax.broadcasted_iota(jnp.int32, (groups, groups), 1)
    strided_visible = far_cols < far_rows

    def band_view(values):
        return values.reshape(blocks_here, BLOCK, heads_here, DH)

    def group_view(values):
        return values.reshape(groups, residues, width_here)

    def strided_view(values):
        return values.reshape(groups, residues, heads_here, DH)

    full_grad = lax.all_gather(out_grad, "head", axis=1, tiled=True)
    grad_rows = lax.dot_general(
        full_grad,
        lax.all_gather(out_weight, "seq", axis=1, tiled=True),
        (((1,), (1,)), ((), ())),
        preferred_element_type=jnp.float32,
    ).astype(jnp.bfloat16)
    strided_query, strided_key, strided_value, strided_grad = (
        lax.all_to_all(group_view(query_rows), "seq", split_axis=0, concat_axis=0, tiled=True),
        lax.all_to_all(group_view(key_rows), "seq", split_axis=0, concat_axis=0, tiled=True),
        lax.all_to_all(group_view(value_rows), "seq", split_axis=0, concat_axis=0, tiled=True),
        lax.all_to_all(group_view(grad_rows), "seq", split_axis=0, concat_axis=0, tiled=True),
    )
    query_band = band_view(query_rows)
    key_band = band_view(key_rows)
    value_band = band_view(value_rows)
    band_scores, max_band, sum_band, out_band = part_forward(
        query_band, key_band, value_band, band_visible, scaling, band_forms
    )
    max_band = max_band.reshape(tokens_here, heads_here)
    sum_band = sum_band.reshape(tokens_here, heads_here)
    out_band = out_band.reshape(tokens_here, heads_here, DH)
    grad_heads = grad_rows.reshape(tokens_here, heads_here, DH)
    dot_band = jnp.sum(grad_heads.astype(jnp.float32) * out_band, axis=-1)
    far_query = strided_view(strided_query)
    far_key = strided_view(strided_key)
    far_value = strided_view(strided_value)
    far_scores, max_far, sum_far, out_far = part_forward(
        far_query, far_key, far_value, strided_visible, scaling, strided_forms
    )
    max_band_split = max_band.reshape(groups, residues, heads_here)
    sum_band_split = sum_band.reshape(groups, residues, heads_here)
    dot_band_split = dot_band.reshape(groups, residues, heads_here)
    home_out, home_max, home_sum, band_max_far, band_sum_far, band_dot_far = (
        lax.all_to_all(out_far, "seq", split_axis=0, concat_axis=0, tiled=True),
        lax.all_to_all(max_far, "seq", split_axis=0, concat_axis=0, tiled=True),
        lax.all_to_all(sum_far, "seq", split_axis=0, concat_axis=0, tiled=True),
        lax.all_to_all(max_band_split, "seq", split_axis=0, concat_axis=0, tiled=True),
        lax.all_to_all(sum_band_split, "seq", split_axis=0, concat_axis=0, tiled=True),
        lax.all_to_all(dot_band_split, "seq", split_axis=0, concat_axis=0, tiled=True),
    )
    home_out = home_out.reshape(tokens_here, heads_here, DH)
    home_max = home_max.reshape(tokens_here, heads_here)
    home_sum = home_sum.reshape(tokens_here, heads_here)
    home_dot = jnp.sum(grad_heads.astype(jnp.float32) * home_out, axis=-1)
    band_factor, far_factor, total, lse_home, delta_home = combine_stats(
        max_band, sum_band, dot_band, home_max, home_sum, home_dot
    )
    attended = (
        ((band_factor[..., None] * out_band + far_factor[..., None] * home_out) / total[..., None])
        .astype(jnp.bfloat16)
        .reshape(tokens_here, width_here)
    )
    far_grad = strided_view(strided_grad)
    far_dot = jnp.sum(far_grad.astype(jnp.float32) * out_far, axis=-1)
    far_stats = combine_stats(band_max_far, band_sum_far, band_dot_far, max_far, sum_far, far_dot)
    band_grads = part_backward(
        band_scores,
        band_visible,
        lse_home.reshape(blocks_here, BLOCK, heads_here),
        delta_home.reshape(blocks_here, BLOCK, heads_here),
        query_band,
        key_band,
        value_band,
        band_view(grad_rows),
        scaling,
        band_forms,
    )
    far_grads = part_backward(
        far_scores,
        strided_visible,
        far_stats[3],
        far_stats[4],
        far_query,
        far_key,
        far_value,
        far_grad,
        scaling,
        strided_forms,
    )
    home_query, home_key, home_value = (
        lax.all_to_all(
            far_grads[0].astype(jnp.bfloat16).reshape(groups, residues, width_here),
            "seq",
            split_axis=0,
            concat_axis=0,
            tiled=True,
        ),
        lax.all_to_all(
            far_grads[1].astype(jnp.bfloat16).reshape(groups, residues, width_here),
            "seq",
            split_axis=0,
            concat_axis=0,
            tiled=True,
        ),
        lax.all_to_all(
            far_grads[2].astype(jnp.bfloat16).reshape(groups, residues, width_here),
            "seq",
            split_axis=0,
            concat_axis=0,
            tiled=True,
        ),
    )
    query_grad = (
        band_grads[0].reshape(tokens_here, width_here)
        + home_query.reshape(tokens_here, width_here).astype(jnp.float32)
    ).astype(jnp.bfloat16)
    key_grad = (
        band_grads[1].reshape(tokens_here, width_here)
        + home_key.reshape(tokens_here, width_here).astype(jnp.float32)
    ).astype(jnp.bfloat16)
    value_grad = (
        band_grads[2].reshape(tokens_here, width_here)
        + home_value.reshape(tokens_here, width_here).astype(jnp.float32)
    ).astype(jnp.bfloat16)
    return (attended, query_grad, key_grad, value_grad)


MESH = pl.DeviceIdType.MESH
STAT = 128
ROWS = 16


def dot_nt(a, b):
    return lax.dot_general(a, b, (((1,), (1,)), ((), ())), preferred_element_type=jnp.float32)


def dot_nn(a, b):
    return lax.dot_general(a, b, (((1,), (0,)), ((), ())), preferred_element_type=jnp.float32)


def dot_tn(a, b):
    return lax.dot_general(a, b, (((0,), (0,)), ((), ())), preferred_element_type=jnp.float32)


def pack_stats(columns):
    rows = columns[0].shape[0]
    lane = lax.broadcasted_iota(jnp.int32, (rows, STAT), 1)
    which = lane % 8
    spread = jnp.zeros((rows, STAT), jnp.float32)
    for index, column in enumerate(columns):
        spread = jnp.where(which == index, column, spread)
    first = spread.astype(jnp.bfloat16).astype(jnp.float32)
    rest = spread - first
    second = rest.astype(jnp.bfloat16).astype(jnp.float32)
    third = rest - second
    packed = jnp.where(lane < 8, first, jnp.where(lane < 16, second, jnp.where(lane < 24, third, 0.0)))
    return packed.astype(jnp.bfloat16)


def unpack_stat(packed, index):
    lane = lax.broadcasted_iota(jnp.int32, packed.shape, 1)
    return jnp.sum(jnp.where(lane % 8 == index, packed, 0.0), axis=1, keepdims=True)


def fused_kernel(
    groups, heads, chunks, planes,
    q, k, v, og, w,
    att_out, dq_out, dk_out, dv_out,
    og_all, w_all, qf, kf, vf, g_home, gf, far_out, home_out, gr_send, gr_home,
    out_band, att_full, lse_keep, s_band, s_far, band_grads, g_early,
    z_send, z_recv, w_send, w_recv, qkv_send, qkv_recv, out_send, out_recv,
    g_send, g_recv, gr_ssem, gr_rsem,
):
    s = lax.axis_index("seq")
    h = lax.axis_index("head")
    width = heads * DH
    scaling = DH ** (-0.5)
    blocks = groups // 2
    block_rows = groups * ROWS
    row = lax.broadcasted_iota(jnp.int32, (block_rows, block_rows), 0)
    col = lax.broadcasted_iota(jnp.int32, (block_rows, block_rows), 1)
    band_mask = col <= row
    far_mask = (row % ROWS == col % ROWS) & (col // ROWS < row // ROWS)

    def remote(src, dst, ssem, rsem, to):
        return pltpu.make_async_remote_copy(
            src_ref=src, dst_ref=dst, send_sem=ssem, recv_sem=rsem, device_id=to, device_id_type=MESH
        )

    core, x, y = s % 2, s // 2 % 2, s // 4

    def other(o):
        return (
            (1 - y if o & 4 else y) * 4 + (1 - x if o & 2 else x) * 2 + (1 - core if o & 1 else core)
        )

    def peer(o):
        return (other(o), h)

    barrier = pltpu.get_barrier_semaphore()
    for o in range(1, groups):
        pl.semaphore_signal(barrier, inc=1, device_id=peer(o), device_id_type=MESH)
    for z in range(planes):
        @pl.when((h == z + 1) | (h == z - 1))
        def _():
            pl.semaphore_signal(barrier, inc=1, device_id=(s, z), device_id_type=MESH)
    inner = (h > 0) & (h < planes - 1)

    @pl.when(inner)
    def _():
        pl.semaphore_wait(barrier, groups + 1)

    @pl.when(jnp.logical_not(inner))
    def _():
        pl.semaphore_wait(barrier, groups)

    def z_copy(slot, c, direction):
        mine = og_all.at[slot, c]
        return remote(mine, mine, z_send.at[direction, slot, c], z_recv.at[slot, c],
                      (s, h + (1 if direction == 0 else -1)))

    def z_own(c, direction):
        return remote(og.at[:, c], og_all.at[h, c], z_send.at[direction, h, c], z_recv.at[h, c],
                      (s, h + (1 if direction == 0 else -1)))

    def z_pass(slot, c):
        @pl.when(h != slot)
        def _():
            z_copy(slot, c, 0).wait_recv()

        @pl.when((h > slot) & (h < planes - 1))
        def _():
            z_copy(slot, c, 0).start()

        @pl.when((h < slot) & (h > 0))
        def _():
            z_copy(slot, c, 1).start()

    @pl.loop(0, chunks)
    def _(c):
        @pl.when(h < planes - 1)
        def _():
            z_own(c, 0).start()

        @pl.when(h > 0)
        def _():
            z_own(c, 1).start()

    half = w.shape[0] // 2
    low, high = pl.ds(0, half), pl.ds(half, half)

    def w_own(index, o):
        return remote(w, w_all.at[s], w_send.at[index], w_recv.at[index], peer(o))

    def w_part(index, source, rows, o):
        ref = w_all.at[source, rows]
        return remote(ref, ref, w_send.at[index], w_recv.at[index], peer(o))

    def qkv_copy(t, src, dst, o):
        return remote(src.at[other(o)], dst.at[:, s], qkv_send.at[t, o], qkv_recv.at[t, o], peer(o))

    triples = ((q, qf), (k, kf), (v, vf))
    for o in (6, 2, 4, 7, 3, 5, 1):
        for t, (src, dst) in enumerate(triples):
            qkv_copy(t, src, dst, o).start()
    for src, dst in triples:
        dst[:, s] = src[s]
    w_all[s] = w[...]

    def forward_block(queries, keys_part, values_part, mask):
        scores = dot_nt(queries, keys_part) * scaling
        row_max = jnp.max(jnp.where(mask, scores, SENTINEL), axis=1, keepdims=True)
        weights = jnp.where(mask, jnp.exp(scores - row_max), 0.0)
        row_sum = jnp.maximum(jnp.sum(weights, axis=1, keepdims=True), 1.0)
        partial = dot_nn(weights.astype(jnp.bfloat16), values_part) / row_sum
        return scores, row_max + jnp.log(row_sum), partial

    def columns(head):
        return slice(head * DH, (head + 1) * DH)

    def natural(ref, b):
        return ref[pl.ds(2 * b, 2)].reshape(block_rows, ref.shape[-1])

    def place(column, head, rows):
        lane = lax.broadcasted_iota(jnp.int32, (rows, STAT), 1)
        return jnp.where(lane == head, column, 0.0)

    @pl.loop(0, blocks)
    def _(b):
        qb, kb, vb = natural(q, b), natural(k, b), natural(v, b)
        kept = jnp.zeros((block_rows, STAT), jnp.float32)
        for head in range(heads):
            at = columns(head)
            scores, lse, partial = forward_block(qb[:, at], kb[:, at], vb[:, at], band_mask)
            s_band[b * heads + head] = scores
            out_band[b, :, at] = partial
            kept = kept + place(lse, head, block_rows)
        lse_keep[pl.ds(2 * b, 2)] = kept.reshape(2, chunks, ROWS, STAT)

    w_first = [w_own(0, 2), w_own(1, 4), w_own(2, 1)]
    for copy in w_first:
        copy.start()

    def z_near(c):
        for slot in range(planes):
            @pl.when((h == slot + 1) | (h == slot - 1))
            def _():
                z_pass(slot, c)

    def z_far(c, distance):
        for slot in range(planes):
            @pl.when((h == slot + distance) | (h == slot - distance))
            def _():
                z_pass(slot, c)

    @pl.loop(0, chunks)
    def _(c):
        z_near(c)

    for o in range(1, groups):
        for t, (src, dst) in enumerate(triples):
            qkv_copy(t, src, dst, o).wait_recv()

    def out_copy(c, o):
        return remote(far_out.at[c, other(o)], home_out.at[s, c], out_send.at[c, o], out_recv.at[c, o], peer(o))

    def out_arrived(c, o):
        return remote(far_out.at[c, other(o)], home_out.at[other(o), c], out_send.at[c, o], out_recv.at[c, o], peer(o))

    def chunk_of(ref, c):
        return ref[c].reshape(block_rows, ref.shape[-1])

    @pl.loop(0, chunks)
    def _(c):
        qb, kb, vb = chunk_of(qf, c), chunk_of(kf, c), chunk_of(vf, c)
        stats = []
        for head in range(heads):
            at = columns(head)
            scores, lse, partial = forward_block(qb[:, at], kb[:, at], vb[:, at], far_mask)
            s_far[c * heads + head] = scores
            far_out[c, :, :, at] = partial.astype(jnp.bfloat16).reshape(groups, ROWS, DH)
            stats.append(lse)
        far_out[c, :, :, width:] = pack_stats(stats).reshape(groups, ROWS, STAT)
        for o in range(1, groups):
            out_copy(c, o).start()
        home_out[s, c] = far_out[c, s]

    w_own(0, 2).wait_recv()
    w_second = [w_part(3, other(2), low, 4), w_part(4, other(2), slice(None), 1)]
    for copy in w_second:
        copy.start()
    w_own(1, 4).wait_recv()
    w_third = [w_part(5, other(4), high, 2), w_part(6, other(4), slice(None), 1)]
    for copy in w_third:
        copy.start()

    w_part(3, other(6), low, 4).wait_recv()
    w_fourth = [w_part(7, other(6), low, 1)]
    w_fourth[0].start()
    w_part(5, other(6), high, 2).wait_recv()
    w_fourth.append(w_part(8, other(6), high, 1))
    w_fourth[1].start()

    @pl.loop(0, chunks)
    def _(c):
        for o in range(1, groups):
            out_arrived(c, o).wait_recv()

    @pl.loop(0, blocks)
    def _(b):
        message = natural(home_out, b)
        packed = message[:, width:].astype(jnp.float32)
        band = natural(lse_keep, b)
        kept = jnp.zeros((block_rows, STAT), jnp.float32)
        for head in range(heads):
            at = columns(head)
            lse_far = unpack_stat(packed, head)
            lse_near = band[:, head:head + 1]
            top = jnp.maximum(lse_far, lse_near)
            near_factor = jnp.exp(lse_near - top)
            far_factor = jnp.exp(lse_far - top)
            total = near_factor + far_factor
            combined = (near_factor * out_band[b, :, at] + far_factor * message[:, at].astype(jnp.float32)) / total
            att_full[pl.ds(2 * b, 2), :, :, at] = combined.reshape(2, chunks, ROWS, DH)
            att_out[pl.ds(2 * b, 2), :, :, at] = combined.astype(jnp.bfloat16).reshape(2, chunks, ROWS, DH)
            kept = kept + place(top + jnp.log(total), head, block_rows)
        lse_keep[pl.ds(2 * b, 2)] = kept.reshape(2, chunks, ROWS, STAT)

    def g_copy(c, o):
        return remote(g_home.at[other(o), c], gf.at[c, s], g_send.at[c, o], g_recv.at[c, o], peer(o))

    def g_arrived(c, o):
        return remote(g_home.at[other(o), c], gf.at[c, other(o)], g_send.at[c, o], g_recv.at[c, o], peer(o))

    def gr_copy(c, o):
        return remote(gr_send.at[c, other(o)], gr_home.at[s, c], gr_ssem.at[c, o], gr_rsem.at[c, o], peer(o))

    def gr_arrived(c, o):
        return remote(gr_send.at[c, other(o)], gr_home.at[other(o), c], gr_ssem.at[c, o], gr_rsem.at[c, o], peer(o))

    @pl.loop(0, chunks)
    def _(c):
        og_all[h, c] = og[:, c]

    per = og.shape[-1] // w.shape[1]
    depth = w.shape[1]
    first = h // 2
    last = (planes - 1) * (1 - first)

    @pl.when(inner)
    def _():
        for c in range(2):
            z_far(c, 2)

    @pl.when(jnp.logical_not(inner))
    def _():
        for c in range(chunks):
            z_far(c, 2)

    w_own(2, 1).wait_recv()
    w_part(4, other(3), slice(None), 1).wait_recv()
    w_part(6, other(5), slice(None), 1).wait_recv()
    w_part(7, other(7), low, 1).wait_recv()
    w_part(8, other(7), high, 1).wait_recv()

    early = jnp.zeros((chunks * block_rows, width), jnp.float32)
    for slot in range(planes - 1):
        for part in range(per):
            left = og_all[first + slot, :, :, :, part * depth:(part + 1) * depth]
            early = early + dot_nt(left.reshape(chunks * block_rows, depth), w_all[(first + slot) * per + part])
    g_early[...] = early.reshape(chunks, block_rows, width)

    def grad_chunk(c):
        @pl.when(inner & (c < chunks - 2))
        def _():
            z_far(c + 2, 2)

        @pl.when(jnp.logical_not(inner))
        def _():
            z_far(c, planes - 1)
        total = g_early[c]
        for part in range(per):
            left = og_all[last, c, :, :, part * depth:(part + 1) * depth]
            total = total + dot_nt(left.reshape(block_rows, depth), w_all[last * per + part])
        grad = total.astype(jnp.bfloat16)
        g_home[:, c, :, :width] = grad.reshape(groups, ROWS, width)
        grad = grad.astype(jnp.float32)
        attended = att_full[:, c].reshape(block_rows, width)
        kept = lse_keep[:, c].reshape(block_rows, STAT)
        stats = [kept[:, head:head + 1] for head in range(heads)]
        stats += [jnp.sum(grad[:, columns(head)] * attended[:, columns(head)], axis=1, keepdims=True) for head in range(heads)]
        g_home[:, c, :, width:] = pack_stats(stats).reshape(groups, ROWS, STAT)
        for o in range(1, groups):
            g_copy(c, o).start()
        gf[c, s] = g_home[s, c]

    def backward_block(scores, mask, lse, delta, queries, keys_part, values_part, grad_part):
        probs = jnp.where(mask, jnp.exp(scores - lse), 0.0)
        value_part = dot_tn(probs.astype(jnp.bfloat16), grad_part)
        dprob = dot_nt(grad_part, values_part)
        dscore = (probs * (dprob - delta)).astype(jnp.bfloat16)
        return dot_nn(dscore, keys_part) * scaling, dot_tn(dscore, queries) * scaling, value_part

    def far_backward(c):
        for o in range(1, groups):
            g_arrived(c, o).wait_recv()
        qb, kb, vb, message = chunk_of(qf, c), chunk_of(kf, c), chunk_of(vf, c), chunk_of(gf, c)
        packed = message[:, width:].astype(jnp.float32)
        for head in range(heads):
            at = columns(head)
            parts = backward_block(
                s_far[c * heads + head], far_mask, unpack_stat(packed, head), unpack_stat(packed, heads + head),
                qb[:, at], kb[:, at], vb[:, at], message[:, at],
            )
            for t, part in enumerate(parts):
                gr_send[c, :, t, :, at] = part.astype(jnp.bfloat16).reshape(groups, ROWS, DH)
        for o in range(1, groups):
            gr_copy(c, o).start()
        gr_home[s, c] = gr_send[c, s]

    @pl.loop(0, chunks + 1)
    def _(c):
        @pl.when(c < chunks)
        def _():
            grad_chunk(c)

        @pl.when(c > 0)
        def _():
            far_backward(c - 1)

    @pl.loop(0, blocks)
    def _(b):
        qb, kb, vb, message = natural(q, b), natural(k, b), natural(v, b), natural(g_home, b)
        packed = message[:, width:].astype(jnp.float32)
        for head in range(heads):
            at = columns(head)
            parts = backward_block(
                s_band[b * heads + head], band_mask, unpack_stat(packed, head), unpack_stat(packed, heads + head),
                qb[:, at], kb[:, at], vb[:, at], message[:, at],
            )
            for t, part in enumerate(parts):
                band_grads[t, b, :, at] = part

    @pl.loop(0, chunks)
    def _(c):
        for o in range(1, groups):
            gr_arrived(c, o).wait_recv()

    @pl.loop(0, blocks)
    def _(b):
        for t, result in enumerate((dq_out, dk_out, dv_out)):
            arrived = gr_home[pl.ds(2 * b, 2), :, t].reshape(block_rows, width).astype(jnp.float32)
            result[pl.ds(2 * b, 2)] = (
                (band_grads[t, b] + arrived).astype(jnp.bfloat16).reshape(2, chunks, ROWS, width)
            )

    for copy in w_first + w_second + w_third + w_fourth:
        copy.wait_send()
    for o in range(1, groups):
        for t, (src, dst) in enumerate(triples):
            qkv_copy(t, src, dst, o).wait_send()

    @pl.loop(0, chunks)
    def _(c):
        for o in range(1, groups):
            out_copy(c, o).wait_send()
            g_copy(c, o).wait_send()
            gr_copy(c, o).wait_send()

        @pl.when(h < planes - 1)
        def _():
            z_own(c, 0).wait_send()

        @pl.when(h > 0)
        def _():
            z_own(c, 1).wait_send()

        for slot in range(planes):
            @pl.when((h > slot) & (h < planes - 1))
            def _():
                z_copy(slot, c, 0).wait_send()

            @pl.when((h < slot) & (h > 0))
            def _():
                z_copy(slot, c, 1).wait_send()


def fused_local(query_rows, key_rows, value_rows, out_grad, out_weight):
    tokens_here, width = query_rows.shape
    heads = width // DH
    groups = lax.axis_size("seq")
    planes = lax.axis_size("head")
    chunks = tokens_here // groups // ROWS
    depth = out_grad.shape[1]
    block_rows = groups * ROWS
    blocks = tokens_here // block_rows

    def split(values):
        return values.reshape(groups, chunks, ROWS, values.shape[1])

    half, full = jnp.bfloat16, jnp.float32
    dma = pltpu.SemaphoreType.DMA
    in_vmem = pl.BlockSpec(memory_space=pltpu.VMEM)
    results = pl.pallas_call(
        functools.partial(fused_kernel, groups, heads, chunks, planes),
        out_shape=[jax.ShapeDtypeStruct((groups, chunks, ROWS, width), half)] * 4,
        in_specs=[in_vmem] * 5,
        out_specs=[in_vmem] * 4,
        scratch_shapes=[
            pltpu.VMEM((planes, chunks, groups, ROWS, depth), half),
            pltpu.VMEM((groups,) + out_weight.shape, half),
            pltpu.VMEM((chunks, groups, ROWS, width), half),
            pltpu.VMEM((chunks, groups, ROWS, width), half),
            pltpu.VMEM((chunks, groups, ROWS, width), half),
            pltpu.VMEM((groups, chunks, ROWS, width + STAT), half),
            pltpu.VMEM((chunks, groups, ROWS, width + STAT), half),
            pltpu.VMEM((chunks, groups, ROWS, width + STAT), half),
            pltpu.VMEM((groups, chunks, ROWS, width + STAT), half),
            pltpu.VMEM((chunks, groups, 3, ROWS, width), half),
            pltpu.VMEM((groups, chunks, 3, ROWS, width), half),
            pltpu.VMEM((blocks, block_rows, width), full),
            pltpu.VMEM((groups, chunks, ROWS, width), full),
            pltpu.VMEM((groups, chunks, ROWS, STAT), full),
            pltpu.VMEM((blocks * heads, block_rows, block_rows), full),
            pltpu.VMEM((chunks * heads, block_rows, block_rows), full),
            pltpu.VMEM((3, blocks, block_rows, width), full),
            pltpu.VMEM((chunks, block_rows, width), full),
            dma((2, planes, chunks)),
            dma((planes, chunks)),
            dma((9,)),
            dma((9,)),
            dma((3, groups)),
            dma((3, groups)),
            dma((chunks, groups)),
            dma((chunks, groups)),
            dma((chunks, groups)),
            dma((chunks, groups)),
            dma((chunks, groups)),
            dma((chunks, groups)),
        ],
        compiler_params=pltpu.CompilerParams(
            collective_id=0, has_side_effects=True, vmem_limit_bytes=56 << 20
        ),
    )(split(query_rows), split(key_rows), split(value_rows), split(out_grad), out_weight)
    return tuple(result.reshape(tokens_here, width) for result in results)


def fits(mesh):
    return mesh.shape["seq"] == 8 and mesh.shape["head"] == 4


def solution(mesh):
    placed = (
        P("seq", "head"),
        P("seq", "head"),
        P("seq", "head"),
        P("seq", "head"),
        P("head", "seq"),
    )
    return jax.shard_map(
        fused_local if fits(mesh) else local,
        mesh=mesh,
        in_specs=placed,
        out_specs=(P("seq", "head"), P("seq", "head"), P("seq", "head"), P("seq", "head")),
        check_vma=False,
    )
```

```python
import functools

import jax
import jax.experimental.pallas as pl
import jax.experimental.pallas.tpu as pltpu
import jax.numpy as jnp
from jax import lax
from jax.sharding import PartitionSpec as P

DH = 128
BLOCK = 128


SENTINEL = -1e30


def part_forward(queries, keys_part, values_part, visible, scaling, layout_forms):
    query_form, key_form, score_form, row_order, score_order = layout_forms
    scores = (
        jnp.einsum(
            query_form + "," + key_form + "->" + score_form,
            queries,
            keys_part,
            preferred_element_type=jnp.float32,
        )
        * scaling
    )
    row_max = jnp.max(jnp.where(visible, scores, SENTINEL), axis=-1)
    weights = jnp.where(visible, jnp.exp(scores - row_max[..., None]), 0.0)
    row_sum = jnp.sum(weights, axis=-1)
    partial_out = jnp.einsum(
        score_form + "," + key_form + "->" + query_form,
        weights.astype(jnp.bfloat16),
        values_part,
        preferred_element_type=jnp.float32,
    )
    return (
        scores,
        jnp.transpose(row_max, row_order),
        jnp.transpose(row_sum, row_order),
        partial_out,
    )


def part_backward(
    scores,
    visible,
    lse_rows,
    delta_rows,
    queries,
    keys_part,
    values_part,
    grad_part,
    scaling,
    layout_forms,
):
    query_form, key_form, score_form, row_order, score_order = layout_forms
    probs = jnp.where(
        visible, jnp.exp(scores - jnp.transpose(lse_rows, score_order)[..., None]), 0.0
    )
    value_part_grad = jnp.einsum(
        score_form + "," + query_form + "->" + key_form,
        probs.astype(jnp.bfloat16),
        grad_part,
        preferred_element_type=jnp.float32,
    )
    dprob = jnp.einsum(
        query_form + "," + key_form + "->" + score_form,
        grad_part,
        values_part,
        preferred_element_type=jnp.float32,
    )
    dscore = (probs * (dprob - jnp.transpose(delta_rows, score_order)[..., None])).astype(
        jnp.bfloat16
    )
    query_part_grad = (
        jnp.einsum(
            score_form + "," + key_form + "->" + query_form,
            dscore,
            keys_part,
            preferred_element_type=jnp.float32,
        )
        * scaling
    )
    key_part_grad = (
        jnp.einsum(
            score_form + "," + query_form + "->" + key_form,
            dscore,
            queries,
            preferred_element_type=jnp.float32,
        )
        * scaling
    )
    return (query_part_grad, key_part_grad, value_part_grad)


def combine_stats(max_band, sum_band, dot_band, max_strided, sum_strided, dot_strided):
    top = jnp.maximum(max_band, max_strided)
    band_factor = jnp.exp(max_band - top)
    strided_factor = jnp.exp(max_strided - top)
    total = band_factor * sum_band + strided_factor * sum_strided
    delta = (band_factor * dot_band + strided_factor * dot_strided) / total
    return (band_factor, strided_factor, total, top + jnp.log(total), delta)


def local(query_rows, key_rows, value_rows, out_grad, out_weight):
    tokens_here, width_here = query_rows.shape
    heads_here = width_here // DH
    groups = lax.axis_size("seq")
    residues = tokens_here // groups
    blocks_here = tokens_here // BLOCK
    scaling = DH ** (-0.5)
    band_forms = ("bihd", "bjhd", "bhij", (0, 2, 1), (0, 2, 1))
    strided_forms = ("ishd", "jshd", "shij", (2, 0, 1), (1, 2, 0))
    band_rows = lax.broadcasted_iota(jnp.int32, (BLOCK, BLOCK), 0)
    band_cols = lax.broadcasted_iota(jnp.int32, (BLOCK, BLOCK), 1)
    band_visible = band_cols <= band_rows
    far_rows = lax.broadcasted_iota(jnp.int32, (groups, groups), 0)
    far_cols = lax.broadcasted_iota(jnp.int32, (groups, groups), 1)
    strided_visible = far_cols < far_rows

    def band_view(values):
        return values.reshape(blocks_here, BLOCK, heads_here, DH)

    def group_view(values):
        return values.reshape(groups, residues, width_here)

    def strided_view(values):
        return values.reshape(groups, residues, heads_here, DH)

    full_grad = lax.all_gather(out_grad, "head", axis=1, tiled=True)
    grad_rows = lax.dot_general(
        full_grad,
        lax.all_gather(out_weight, "seq", axis=1, tiled=True),
        (((1,), (1,)), ((), ())),
        preferred_element_type=jnp.float32,
    ).astype(jnp.bfloat16)
    strided_query, strided_key, strided_value, strided_grad = (
        lax.all_to_all(group_view(query_rows), "seq", split_axis=0, concat_axis=0, tiled=True),
        lax.all_to_all(group_view(key_rows), "seq", split_axis=0, concat_axis=0, tiled=True),
        lax.all_to_all(group_view(value_rows), "seq", split_axis=0, concat_axis=0, tiled=True),
        lax.all_to_all(group_view(grad_rows), "seq", split_axis=0, concat_axis=0, tiled=True),
    )
    query_band = band_view(query_rows)
    key_band = band_view(key_rows)
    value_band = band_view(value_rows)
    band_scores, max_band, sum_band, out_band = part_forward(
        query_band, key_band, value_band, band_visible, scaling, band_forms
    )
    max_band = max_band.reshape(tokens_here, heads_here)
    sum_band = sum_band.reshape(tokens_here, heads_here)
    out_band = out_band.reshape(tokens_here, heads_here, DH)
    grad_heads = grad_rows.reshape(tokens_here, heads_here, DH)
    dot_band = jnp.sum(grad_heads.astype(jnp.float32) * out_band, axis=-1)
    far_query = strided_view(strided_query)
    far_key = strided_view(strided_key)
    far_value = strided_view(strided_value)
    far_scores, max_far, sum_far, out_far = part_forward(
        far_query, far_key, far_value, strided_visible, scaling, strided_forms
    )
    max_band_split = max_band.reshape(groups, residues, heads_here)
    sum_band_split = sum_band.reshape(groups, residues, heads_here)
    dot_band_split = dot_band.reshape(groups, residues, heads_here)
    home_out, home_max, home_sum, band_max_far, band_sum_far, band_dot_far = (
        lax.all_to_all(out_far, "seq", split_axis=0, concat_axis=0, tiled=True),
        lax.all_to_all(max_far, "seq", split_axis=0, concat_axis=0, tiled=True),
        lax.all_to_all(sum_far, "seq", split_axis=0, concat_axis=0, tiled=True),
        lax.all_to_all(max_band_split, "seq", split_axis=0, concat_axis=0, tiled=True),
        lax.all_to_all(sum_band_split, "seq", split_axis=0, concat_axis=0, tiled=True),
        lax.all_to_all(dot_band_split, "seq", split_axis=0, concat_axis=0, tiled=True),
    )
    home_out = home_out.reshape(tokens_here, heads_here, DH)
    home_max = home_max.reshape(tokens_here, heads_here)
    home_sum = home_sum.reshape(tokens_here, heads_here)
    home_dot = jnp.sum(grad_heads.astype(jnp.float32) * home_out, axis=-1)
    band_factor, far_factor, total, lse_home, delta_home = combine_stats(
        max_band, sum_band, dot_band, home_max, home_sum, home_dot
    )
    attended = (
        ((band_factor[..., None] * out_band + far_factor[..., None] * home_out) / total[..., None])
        .astype(jnp.bfloat16)
        .reshape(tokens_here, width_here)
    )
    far_grad = strided_view(strided_grad)
    far_dot = jnp.sum(far_grad.astype(jnp.float32) * out_far, axis=-1)
    far_stats = combine_stats(band_max_far, band_sum_far, band_dot_far, max_far, sum_far, far_dot)
    band_grads = part_backward(
        band_scores,
        band_visible,
        lse_home.reshape(blocks_here, BLOCK, heads_here),
        delta_home.reshape(blocks_here, BLOCK, heads_here),
        query_band,
        key_band,
        value_band,
        band_view(grad_rows),
        scaling,
        band_forms,
    )
    far_grads = part_backward(
        far_scores,
        strided_visible,
        far_stats[3],
        far_stats[4],
        far_query,
        far_key,
        far_value,
        far_grad,
        scaling,
        strided_forms,
    )
    home_query, home_key, home_value = (
        lax.all_to_all(
            far_grads[0].astype(jnp.bfloat16).reshape(groups, residues, width_here),
            "seq",
            split_axis=0,
            concat_axis=0,
            tiled=True,
        ),
        lax.all_to_all(
            far_grads[1].astype(jnp.bfloat16).reshape(groups, residues, width_here),
            "seq",
            split_axis=0,
            concat_axis=0,
            tiled=True,
        ),
        lax.all_to_all(
            far_grads[2].astype(jnp.bfloat16).reshape(groups, residues, width_here),
            "seq",
            split_axis=0,
            concat_axis=0,
            tiled=True,
        ),
    )
    query_grad = (
        band_grads[0].reshape(tokens_here, width_here)
        + home_query.reshape(tokens_here, width_here).astype(jnp.float32)
    ).astype(jnp.bfloat16)
    key_grad = (
        band_grads[1].reshape(tokens_here, width_here)
        + home_key.reshape(tokens_here, width_here).astype(jnp.float32)
    ).astype(jnp.bfloat16)
    value_grad = (
        band_grads[2].reshape(tokens_here, width_here)
        + home_value.reshape(tokens_here, width_here).astype(jnp.float32)
    ).astype(jnp.bfloat16)
    return (attended, query_grad, key_grad, value_grad)


MESH = pl.DeviceIdType.MESH
STAT = 128
ROWS = 16


def dot_nt(a, b):
    return lax.dot_general(a, b, (((1,), (1,)), ((), ())), preferred_element_type=jnp.float32)


def dot_nn(a, b):
    return lax.dot_general(a, b, (((1,), (0,)), ((), ())), preferred_element_type=jnp.float32)


def dot_tn(a, b):
    return lax.dot_general(a, b, (((0,), (0,)), ((), ())), preferred_element_type=jnp.float32)


def pack_stats(columns):
    rows = columns[0].shape[0]
    lane = lax.broadcasted_iota(jnp.int32, (rows, STAT), 1)
    which = lane % 8
    spread = jnp.zeros((rows, STAT), jnp.float32)
    for index, column in enumerate(columns):
        spread = jnp.where(which == index, column, spread)
    first = spread.astype(jnp.bfloat16).astype(jnp.float32)
    rest = spread - first
    second = rest.astype(jnp.bfloat16).astype(jnp.float32)
    third = rest - second
    packed = jnp.where(lane < 8, first, jnp.where(lane < 16, second, jnp.where(lane < 24, third, 0.0)))
    return packed.astype(jnp.bfloat16)


def unpack_stat(packed, index):
    lane = lax.broadcasted_iota(jnp.int32, packed.shape, 1)
    return jnp.sum(jnp.where(lane % 8 == index, packed, 0.0), axis=1, keepdims=True)


def fused_kernel(
    groups, heads, chunks, planes,
    q, k, v, og, w,
    att_out, dq_out, dk_out, dv_out,
    og_all, w_all, qf, kf, vf, g_home, gf, far_out, home_out, gr_send, gr_home,
    out_band, att_full, lse_keep, s_band, s_far, band_grads, g_early,
    z_send, z_recv, w_send, w_recv, qkv_send, qkv_recv, out_send, out_recv,
    g_send, g_recv, gr_ssem, gr_rsem,
):
    s = lax.axis_index("seq")
    h = lax.axis_index("head")
    width = heads * DH
    scaling = DH ** (-0.5)
    blocks = groups // 2
    block_rows = groups * ROWS
    row = lax.broadcasted_iota(jnp.int32, (block_rows, block_rows), 0)
    col = lax.broadcasted_iota(jnp.int32, (block_rows, block_rows), 1)
    band_mask = col <= row
    far_mask = (row % ROWS == col % ROWS) & (col // ROWS < row // ROWS)

    def remote(src, dst, ssem, rsem, to):
        return pltpu.make_async_remote_copy(
            src_ref=src, dst_ref=dst, send_sem=ssem, recv_sem=rsem, device_id=to, device_id_type=MESH
        )

    core, x, y = s % 2, s // 2 % 2, s // 4

    def other(o):
        return (
            (1 - y if o & 4 else y) * 4 + (1 - x if o & 2 else x) * 2 + (1 - core if o & 1 else core)
        )

    def peer(o):
        return (other(o), h)

    barrier = pltpu.get_barrier_semaphore()
    for o in range(1, groups):
        pl.semaphore_signal(barrier, inc=1, device_id=peer(o), device_id_type=MESH)
    for z in range(planes):
        @pl.when((h == z + 1) | (h == z - 1))
        def _():
            pl.semaphore_signal(barrier, inc=1, device_id=(s, z), device_id_type=MESH)
    inner = (h > 0) & (h < planes - 1)

    @pl.when(inner)
    def _():
        pl.semaphore_wait(barrier, groups + 1)

    @pl.when(jnp.logical_not(inner))
    def _():
        pl.semaphore_wait(barrier, groups)

    def z_copy(slot, c, direction):
        mine = og_all.at[slot, c]
        return remote(mine, mine, z_send.at[direction, slot, c], z_recv.at[slot, c],
                      (s, h + (1 if direction == 0 else -1)))

    def z_own(c, direction):
        return remote(og.at[:, c], og_all.at[h, c], z_send.at[direction, h, c], z_recv.at[h, c],
                      (s, h + (1 if direction == 0 else -1)))

    def z_pass(slot, c):
        @pl.when(h != slot)
        def _():
            z_copy(slot, c, 0).wait_recv()

        @pl.when((h > slot) & (h < planes - 1))
        def _():
            z_copy(slot, c, 0).start()

        @pl.when((h < slot) & (h > 0))
        def _():
            z_copy(slot, c, 1).start()

    @pl.loop(0, chunks)
    def _(c):
        @pl.when(h < planes - 1)
        def _():
            z_own(c, 0).start()

        @pl.when(h > 0)
        def _():
            z_own(c, 1).start()

    half = w.shape[0] // 2
    low, high = pl.ds(0, half), pl.ds(half, half)

    def w_own(index, o):
        return remote(w, w_all.at[s], w_send.at[index], w_recv.at[index], peer(o))

    def w_part(index, source, rows, o):
        ref = w_all.at[source, rows]
        return remote(ref, ref, w_send.at[index], w_recv.at[index], peer(o))

    def qkv_copy(t, src, dst, o):
        return remote(src.at[other(o)], dst.at[:, s], qkv_send.at[t, o], qkv_recv.at[t, o], peer(o))

    triples = ((q, qf), (k, kf), (v, vf))
    for o in (6, 2, 4, 7, 3, 5, 1):
        for t, (src, dst) in enumerate(triples):
            qkv_copy(t, src, dst, o).start()
    for src, dst in triples:
        dst[:, s] = src[s]
    w_all[s] = w[...]

    def forward_block(queries, keys_part, values_part, mask):
        scores = dot_nt(queries, keys_part) * scaling
        row_max = jnp.max(jnp.where(mask, scores, SENTINEL), axis=1, keepdims=True)
        weights = jnp.where(mask, jnp.exp(scores - row_max), 0.0)
        row_sum = jnp.maximum(jnp.sum(weights, axis=1, keepdims=True), 1.0)
        partial = dot_nn(weights.astype(jnp.bfloat16), values_part) / row_sum
        return scores, row_max + jnp.log(row_sum), partial

    def columns(head):
        return slice(head * DH, (head + 1) * DH)

    def natural(ref, b):
        return ref[pl.ds(2 * b, 2)].reshape(block_rows, ref.shape[-1])

    def place(column, head, rows):
        lane = lax.broadcasted_iota(jnp.int32, (rows, STAT), 1)
        return jnp.where(lane == head, column, 0.0)

    @pl.loop(0, blocks)
    def _(b):
        qb, kb, vb = natural(q, b), natural(k, b), natural(v, b)
        kept = jnp.zeros((block_rows, STAT), jnp.float32)
        for head in range(heads):
            at = columns(head)
            scores, lse, partial = forward_block(qb[:, at], kb[:, at], vb[:, at], band_mask)
            s_band[b * heads + head] = scores
            out_band[b, :, at] = partial
            kept = kept + place(lse, head, block_rows)
        lse_keep[pl.ds(2 * b, 2)] = kept.reshape(2, chunks, ROWS, STAT)

    w_first = [w_own(0, 2), w_own(1, 4), w_own(2, 1)]
    for copy in w_first:
        copy.start()

    def z_near(c):
        for slot in range(planes):
            @pl.when((h == slot + 1) | (h == slot - 1))
            def _():
                z_pass(slot, c)

    def z_far(c, distance):
        for slot in range(planes):
            @pl.when((h == slot + distance) | (h == slot - distance))
            def _():
                z_pass(slot, c)

    @pl.loop(0, chunks)
    def _(c):
        z_near(c)

    for o in range(1, groups):
        for t, (src, dst) in enumerate(triples):
            qkv_copy(t, src, dst, o).wait_recv()

    def out_copy(c, o):
        return remote(far_out.at[c, other(o)], home_out.at[s, c], out_send.at[c, o], out_recv.at[c, o], peer(o))

    def out_arrived(c, o):
        return remote(far_out.at[c, other(o)], home_out.at[other(o), c], out_send.at[c, o], out_recv.at[c, o], peer(o))

    def chunk_of(ref, c):
        return ref[c].reshape(block_rows, ref.shape[-1])

    @pl.loop(0, chunks)
    def _(c):
        qb, kb, vb = chunk_of(qf, c), chunk_of(kf, c), chunk_of(vf, c)
        stats = []
        for head in range(heads):
            at = columns(head)
            scores, lse, partial = forward_block(qb[:, at], kb[:, at], vb[:, at], far_mask)
            s_far[c * heads + head] = scores
            far_out[c, :, :, at] = partial.astype(jnp.bfloat16).reshape(groups, ROWS, DH)
            stats.append(lse)
        far_out[c, :, :, width:] = pack_stats(stats).reshape(groups, ROWS, STAT)
        for o in range(1, groups):
            out_copy(c, o).start()
        home_out[s, c] = far_out[c, s]

    w_own(0, 2).wait_recv()
    w_second = [w_part(3, other(2), low, 4), w_part(4, other(2), slice(None), 1)]
    for copy in w_second:
        copy.start()
    w_own(1, 4).wait_recv()
    w_third = [w_part(5, other(4), high, 2), w_part(6, other(4), slice(None), 1)]
    for copy in w_third:
        copy.start()

    w_part(3, other(6), low, 4).wait_recv()
    w_fourth = [w_part(7, other(6), low, 1)]
    w_fourth[0].start()
    w_part(5, other(6), high, 2).wait_recv()
    w_fourth.append(w_part(8, other(6), high, 1))
    w_fourth[1].start()

    @pl.when(inner)
    def _():
        for c in range(2):
            z_far(c, 2)

    @pl.loop(0, chunks)
    def _(c):
        for o in range(1, groups):
            out_arrived(c, o).wait_recv()

    @pl.loop(0, blocks)
    def _(b):
        message = natural(home_out, b)
        packed = message[:, width:].astype(jnp.float32)
        band = natural(lse_keep, b)
        kept = jnp.zeros((block_rows, STAT), jnp.float32)
        for head in range(heads):
            at = columns(head)
            lse_far = unpack_stat(packed, head)
            lse_near = band[:, head:head + 1]
            top = jnp.maximum(lse_far, lse_near)
            near_factor = jnp.exp(lse_near - top)
            far_factor = jnp.exp(lse_far - top)
            total = near_factor + far_factor
            combined = (near_factor * out_band[b, :, at] + far_factor * message[:, at].astype(jnp.float32)) / total
            att_full[pl.ds(2 * b, 2), :, :, at] = combined.reshape(2, chunks, ROWS, DH)
            att_out[pl.ds(2 * b, 2), :, :, at] = combined.astype(jnp.bfloat16).reshape(2, chunks, ROWS, DH)
            kept = kept + place(top + jnp.log(total), head, block_rows)
        lse_keep[pl.ds(2 * b, 2)] = kept.reshape(2, chunks, ROWS, STAT)

    def g_copy(c, o):
        return remote(g_home.at[other(o), c], gf.at[c, s], g_send.at[c, o], g_recv.at[c, o], peer(o))

    def g_arrived(c, o):
        return remote(g_home.at[other(o), c], gf.at[c, other(o)], g_send.at[c, o], g_recv.at[c, o], peer(o))

    def gr_copy(c, o):
        return remote(gr_send.at[c, other(o)], gr_home.at[s, c], gr_ssem.at[c, o], gr_rsem.at[c, o], peer(o))

    def gr_arrived(c, o):
        return remote(gr_send.at[c, other(o)], gr_home.at[other(o), c], gr_ssem.at[c, o], gr_rsem.at[c, o], peer(o))

    @pl.loop(0, chunks)
    def _(c):
        og_all[h, c] = og[:, c]

    per = og.shape[-1] // w.shape[1]
    depth = w.shape[1]
    first = h // 2
    last = (planes - 1) * (1 - first)

    @pl.when(jnp.logical_not(inner))
    def _():
        for c in range(chunks):
            z_far(c, 2)

    w_own(2, 1).wait_recv()
    w_part(4, other(3), slice(None), 1).wait_recv()
    w_part(6, other(5), slice(None), 1).wait_recv()
    w_part(7, other(7), low, 1).wait_recv()
    w_part(8, other(7), high, 1).wait_recv()

    early = jnp.zeros((chunks * block_rows, width), jnp.float32)
    for slot in range(planes - 1):
        for part in range(per):
            left = og_all[first + slot, :, :, :, part * depth:(part + 1) * depth]
            early = early + dot_nt(left.reshape(chunks * block_rows, depth), w_all[(first + slot) * per + part])
    g_early[...] = early.reshape(chunks, block_rows, width)

    def grad_chunk(c):
        @pl.when(inner & (c < chunks - 2))
        def _():
            z_far(c + 2, 2)

        @pl.when(jnp.logical_not(inner))
        def _():
            z_far(c, planes - 1)
        total = g_early[c]
        for part in range(per):
            left = og_all[last, c, :, :, part * depth:(part + 1) * depth]
            total = total + dot_nt(left.reshape(block_rows, depth), w_all[last * per + part])
        grad = total.astype(jnp.bfloat16)
        g_home[:, c, :, :width] = grad.reshape(groups, ROWS, width)
        grad = grad.astype(jnp.float32)
        attended = att_full[:, c].reshape(block_rows, width)
        kept = lse_keep[:, c].reshape(block_rows, STAT)
        stats = [kept[:, head:head + 1] for head in range(heads)]
        stats += [jnp.sum(grad[:, columns(head)] * attended[:, columns(head)], axis=1, keepdims=True) for head in range(heads)]
        g_home[:, c, :, width:] = pack_stats(stats).reshape(groups, ROWS, STAT)
        for o in range(1, groups):
            g_copy(c, o).start()
        gf[c, s] = g_home[s, c]

    def backward_block(scores, mask, lse, delta, queries, keys_part, values_part, grad_part):
        probs = jnp.where(mask, jnp.exp(scores - lse), 0.0)
        value_part = dot_tn(probs.astype(jnp.bfloat16), grad_part)
        dprob = dot_nt(grad_part, values_part)
        dscore = (probs * (dprob - delta)).astype(jnp.bfloat16)
        return dot_nn(dscore, keys_part) * scaling, dot_tn(dscore, queries) * scaling, value_part

    def far_backward(c):
        for o in range(1, groups):
            g_arrived(c, o).wait_recv()
        qb, kb, vb, message = chunk_of(qf, c), chunk_of(kf, c), chunk_of(vf, c), chunk_of(gf, c)
        packed = message[:, width:].astype(jnp.float32)
        for head in range(heads):
            at = columns(head)
            parts = backward_block(
                s_far[c * heads + head], far_mask, unpack_stat(packed, head), unpack_stat(packed, heads + head),
                qb[:, at], kb[:, at], vb[:, at], message[:, at],
            )
            for t, part in enumerate(parts):
                gr_send[c, :, t, :, at] = part.astype(jnp.bfloat16).reshape(groups, ROWS, DH)
        for o in range(1, groups):
            gr_copy(c, o).start()
        gr_home[s, c] = gr_send[c, s]

    @pl.loop(0, chunks + 1)
    def _(c):
        @pl.when(c < chunks)
        def _():
            grad_chunk(c)

        @pl.when(c > 0)
        def _():
            far_backward(c - 1)

    @pl.loop(0, blocks)
    def _(b):
        qb, kb, vb, message = natural(q, b), natural(k, b), natural(v, b), natural(g_home, b)
        packed = message[:, width:].astype(jnp.float32)
        for head in range(heads):
            at = columns(head)
            parts = backward_block(
                s_band[b * heads + head], band_mask, unpack_stat(packed, head), unpack_stat(packed, heads + head),
                qb[:, at], kb[:, at], vb[:, at], message[:, at],
            )
            for t, part in enumerate(parts):
                band_grads[t, b, :, at] = part

    @pl.loop(0, chunks)
    def _(c):
        for o in range(1, groups):
            gr_arrived(c, o).wait_recv()

    @pl.loop(0, blocks)
    def _(b):
        for t, result in enumerate((dq_out, dk_out, dv_out)):
            arrived = gr_home[pl.ds(2 * b, 2), :, t].reshape(block_rows, width).astype(jnp.float32)
            result[pl.ds(2 * b, 2)] = (
                (band_grads[t, b] + arrived).astype(jnp.bfloat16).reshape(2, chunks, ROWS, width)
            )

    for copy in w_first + w_second + w_third + w_fourth:
        copy.wait_send()
    for o in range(1, groups):
        for t, (src, dst) in enumerate(triples):
            qkv_copy(t, src, dst, o).wait_send()

    @pl.loop(0, chunks)
    def _(c):
        for o in range(1, groups):
            out_copy(c, o).wait_send()
            g_copy(c, o).wait_send()
            gr_copy(c, o).wait_send()

        @pl.when(h < planes - 1)
        def _():
            z_own(c, 0).wait_send()

        @pl.when(h > 0)
        def _():
            z_own(c, 1).wait_send()

        for slot in range(planes):
            @pl.when((h > slot) & (h < planes - 1))
            def _():
                z_copy(slot, c, 0).wait_send()

            @pl.when((h < slot) & (h > 0))
            def _():
                z_copy(slot, c, 1).wait_send()


def settle_kernel(a, b, c, d, a_out, b_out, c_out, d_out, sems):
    copies = [
        pltpu.make_async_copy(source, target, sems.at[index])
        for index, (source, target) in enumerate(((a, a_out), (b, b_out), (c, c_out), (d, d_out)))
    ]
    for copy in copies:
        copy.start()
    for copy in copies:
        copy.wait()


def fused_local(query_rows, key_rows, value_rows, out_grad, out_weight):
    tokens_here, width = query_rows.shape
    heads = width // DH
    groups = lax.axis_size("seq")
    planes = lax.axis_size("head")
    chunks = tokens_here // groups // ROWS
    depth = out_grad.shape[1]
    block_rows = groups * ROWS
    blocks = tokens_here // block_rows

    def split(values):
        return values.reshape(groups, chunks, ROWS, values.shape[1])

    half, full = jnp.bfloat16, jnp.float32
    dma = pltpu.SemaphoreType.DMA
    in_vmem = pl.BlockSpec(memory_space=pltpu.VMEM)
    results = pl.pallas_call(
        functools.partial(fused_kernel, groups, heads, chunks, planes),
        out_shape=[jax.ShapeDtypeStruct((groups, chunks, ROWS, width), half)] * 4,
        in_specs=[in_vmem] * 5,
        out_specs=[in_vmem] * 4,
        scratch_shapes=[
            pltpu.VMEM((planes, chunks, groups, ROWS, depth), half),
            pltpu.VMEM((groups,) + out_weight.shape, half),
            pltpu.VMEM((chunks, groups, ROWS, width), half),
            pltpu.VMEM((chunks, groups, ROWS, width), half),
            pltpu.VMEM((chunks, groups, ROWS, width), half),
            pltpu.VMEM((groups, chunks, ROWS, width + STAT), half),
            pltpu.VMEM((chunks, groups, ROWS, width + STAT), half),
            pltpu.VMEM((chunks, groups, ROWS, width + STAT), half),
            pltpu.VMEM((groups, chunks, ROWS, width + STAT), half),
            pltpu.VMEM((chunks, groups, 3, ROWS, width), half),
            pltpu.VMEM((groups, chunks, 3, ROWS, width), half),
            pltpu.VMEM((blocks, block_rows, width), full),
            pltpu.VMEM((groups, chunks, ROWS, width), full),
            pltpu.VMEM((groups, chunks, ROWS, STAT), full),
            pltpu.VMEM((blocks * heads, block_rows, block_rows), full),
            pltpu.VMEM((chunks * heads, block_rows, block_rows), full),
            pltpu.VMEM((3, blocks, block_rows, width), full),
            pltpu.VMEM((chunks, block_rows, width), full),
            dma((2, planes, chunks)),
            dma((planes, chunks)),
            dma((9,)),
            dma((9,)),
            dma((3, groups)),
            dma((3, groups)),
            dma((chunks, groups)),
            dma((chunks, groups)),
            dma((chunks, groups)),
            dma((chunks, groups)),
            dma((chunks, groups)),
            dma((chunks, groups)),
        ],
        compiler_params=pltpu.CompilerParams(
            collective_id=0, has_side_effects=True, vmem_limit_bytes=56 << 20
        ),
    )(split(query_rows), split(key_rows), split(value_rows), split(out_grad), out_weight)
    anywhere = pl.BlockSpec(memory_space=pl.ANY)
    results = pl.pallas_call(
        settle_kernel,
        out_shape=[jax.ShapeDtypeStruct(result.shape, half) for result in results],
        in_specs=[in_vmem] * 4,
        out_specs=[anywhere] * 4,
        scratch_shapes=[dma((4,))],
    )(*results)
    return tuple(result.reshape(tokens_here, width) for result in results)


def fits(mesh):
    return mesh.shape["seq"] == 8 and mesh.shape["head"] == 4


def solution(mesh):
    placed = (
        P("seq", "head"),
        P("seq", "head"),
        P("seq", "head"),
        P("seq", "head"),
        P("head", "seq"),
    )
    return jax.shard_map(
        fused_local if fits(mesh) else local,
        mesh=mesh,
        in_specs=placed,
        out_specs=(P("seq", "head"), P("seq", "head"), P("seq", "head"), P("seq", "head")),
        check_vma=False,
    )
```
